32 devices in a mesh: section: 2 (over y), expert: 16 (over z, x, core).
Axes of the slice: x: 2, y: 2, z: 4, core: 2. Of those that a mesh axis runs over, the one named last changes fastest.
Arguments:
- acts: bfloat16 [2, 4, 512, 1024], P('section', None, 'expert'), may hold values from -6 to 6
- carried: bfloat16 [2, 512, 1024], P('section', 'expert'), may hold values from -6 to 6
- loss_grad: bfloat16 [4, 512, 1024], P(None, 'expert'), may hold values from -6 to 6
- expert_ids: int32 [2, 4, 512, 8], P('section', None, 'expert'), may hold values from 0 to 15, all different within a row; in each aligned block of 32 rows (0 to 31, 32 to 63, ..., all dimensions but the last counted through in order) at most 24 rows name the same one
- probs: float32 [2, 4, 512, 8], P('section', None, 'expert'), may hold values from 0.1 to 0.4
- w_gate: bfloat16 [2, 16, 1024, 384], P('section', 'expert'), may hold values from -0.1875 to 0.1875
- w_up: bfloat16 [2, 16, 1024, 384], P('section', 'expert'), may hold values from -0.1875 to 0.1875
- w_down: bfloat16 [2, 16, 384, 1024], P('section', 'expert'), may hold values from -0.3125 to 0.3125
Outputs:
- out_grad: bfloat16 [2, 4, 512, 1024], P('section', None, 'expert')
- down_grad: bfloat16 [2, 16, 384, 1024], P('section', 'expert')
The draws below stay inside these ranges and needn't reach their ends.
Inputs may be any that keep to these rules, and one draw needn't show every extreme that they name: `expert_ids`: in each aligned block of 32 tokens of one section and tick, no expert is named by more than 24 of the block's pairs, and in every draw some block has an expert named by exactly 24.
All inputs are finite; a program needn't handle non-finite values.
Results may differ from the reference program's by a relative error of at most 0.0095.
Values may be sent and summed in bfloat16 or wider, within the bound.
A program may use at most 64 MiB of HBM per device.

```python
import math
import jax
import jax.numpy as jnp
import numpy as np
from jax import lax

D = 1024
FF = 384
TOPK = 8
TICKS = 4
TOK = 32
SECTIONS = 2
EXPERTS = 16
TOKENS = 512
SLOT = 24


def levels(rng, shape, shards, low, top_value):
    def one(dim, shards_of):
        steps = jax.random.uniform(jax.random.fold_in(jax.random.fold_in(rng, 6), dim), (shards_of,), jnp.float32, low / len(shards), top_value / len(shards))
        return jnp.repeat(jnp.exp(steps), shape[dim] // shards_of).reshape((-1,) + (1,) * (len(shape) - dim - 1))

    gain = one(*shards[0])
    for cut in shards[1:]:
        gain = gain * one(*cut)
    return gain


def deal_out(rng, own, number, rows, amount, top, bound, lean):
    ranking = jax.random.permutation(rng, amount)
    heavy_load, usual = shares(amount, rows * top, bound, lean, True), shares(amount, rows * top, bound, lean, False)
    places = jnp.arange(amount)

    def named(sizes, offset_by):
        used = int((sizes > 0).sum())
        fixed = max(1, used // 4)
        shifted = fixed + (places - fixed + offset_by * (used - fixed)) % max(1, amount - fixed)
        return jnp.zeros((amount,), jnp.int32).at[ranking[jnp.where(places < fixed, places, shifted)]].set(jnp.asarray(sizes, jnp.int32))

    sizes = jnp.where(number % 4 == 0, named(heavy_load, number // 4), named(usual, number - number // 4 - 1))
    mixed = jax.random.permutation(jax.random.fold_in(own, 3), amount)
    giver, receiver = mixed[0:amount // 2 * 2:2], mixed[1:amount // 2 * 2:2]
    slack = jnp.minimum(sizes[giver] - 1, bound - sizes[receiver]) // 2
    slack = jnp.where((giver == ranking[0]) | (receiver == ranking[0]) | (sizes[receiver] == 0), 0, jnp.maximum(slack, 0))
    shifted = jax.random.randint(jax.random.fold_in(own, 4), (amount // 2,), 0, 1 << 20) % (slack + 1)
    sizes = sizes.at[giver].add(-shifted).at[receiver].add(shifted)
    members = jnp.searchsorted(jnp.cumsum(sizes), jnp.arange(rows * top), side="right").astype(jnp.int32)
    listing = members.reshape(top, rows).T
    listing = listing[jax.random.permutation(jax.random.fold_in(own, 1), rows)]
    offset_by = jax.random.randint(jax.random.fold_in(own, 2), (rows, 1), 0, top)
    return jnp.take_along_axis(listing, (jnp.arange(top)[None, :] + offset_by) % top, axis=1)


def shares(count, total, reach, lean, full):
    loads = [(1 << 20) // math.isqrt(grade ** lean) + 1 for grade in range(1, count + 1)]
    largest = reach if full else min(reach, max(-(-total // count), total * loads[0] // sum(loads)))
    least = 1 if total - largest >= count - 1 else 0
    given, spare = [largest] + [least] * (count - 1), total - largest - least * (count - 1)
    while spare > 0:
        movable = [i for i in range(1, count) if given[i] < largest] or [i for i in range(1, count) if given[i] < reach]
        pool, left = sum([loads[i] for i in movable]), spare
        for i in movable:
            more = min(reach - given[i], max(1, left * loads[i] // pool), spare)
            given[i] = given[i] + more
            spare = spare - more
    return np.array(given)


def bell_draw(own_key, dims, spread, bound, split=(), held_as=jnp.bfloat16):
    factor_of = levels(own_key, dims, split, -0.22, 0.18) if split else 1.0
    values = jax.random.normal(own_key, dims, jnp.float32) * spread * factor_of
    return jnp.minimum(jnp.maximum(values, -bound), bound).astype(held_as)


def setup_inputs(seed: int = 0) -> dict:
    key_of = jax.random.split(jax.random.key(seed), 9)
    acts = bell_draw(key_of[0], (SECTIONS, TICKS, TOKENS, D), 1.0, 6.0, ((0, 2), (2, 16)))
    carried = bell_draw(key_of[1], (SECTIONS, TOKENS, D), 1.0, 6.0, ((0, 2), (1, 16)))
    loss_grad = bell_draw(key_of[2], (TICKS, TOKENS, D), 1.0, 6.0, ((1, 16),))
    expert_ids_keys = jax.random.split(jax.random.fold_in(key_of[3], 1), SECTIONS * TICKS * TOKENS // TOK)
    expert_ids_turns = jax.random.permutation(jax.random.fold_in(key_of[3], 3), SECTIONS * TICKS * TOKENS // TOK)
    expert_ids = jax.vmap(lambda own, number: deal_out(jax.random.fold_in(key_of[3], 2), own, number, TOK, EXPERTS, TOPK, SLOT, 2))(expert_ids_keys, expert_ids_turns).reshape((SECTIONS, TICKS, TOKENS, TOPK))
    probs = jnp.clip(0.1 + 0.3 * jax.random.uniform(key_of[4], (SECTIONS, TICKS, TOKENS, TOPK), jnp.float32) ** levels(key_of[4], (SECTIONS, TICKS, TOKENS, TOPK), ((0, 2), (2, 16)), -0.2, 0.2), 0.1, 0.4)
    w_gate = bell_draw(key_of[5], (SECTIONS, EXPERTS, D, FF), D ** -0.5, 0.1875, ((0, 2), (1, 16)))
    w_up = bell_draw(key_of[6], (SECTIONS, EXPERTS, D, FF), D ** -0.5, 0.1875, ((0, 2), (1, 16)))
    w_down = bell_draw(key_of[7], (SECTIONS, EXPERTS, FF, D), FF ** -0.5, 0.3125, ((0, 2), (1, 16)))
    return dict(acts=acts, carried=carried, loss_grad=loss_grad, expert_ids=expert_ids, probs=probs, w_gate=w_gate, w_up=w_up, w_down=w_down)


def slot_layout(expert_ids):
    tokens_all = expert_ids.shape[0]
    sources = tokens_all // TOK
    onehot = (expert_ids[:, :, None] == jnp.arange(EXPERTS, dtype=jnp.int32)[None, None, :]).astype(jnp.int32)
    blocks = onehot.reshape(sources, TOK * TOPK, EXPERTS)
    before = (jnp.cumsum(blocks, axis=1) - blocks).astype(jnp.int32)
    position = jnp.sum(before * blocks, axis=2).astype(jnp.int32).reshape(tokens_all, TOPK)
    source = (jnp.arange(tokens_all, dtype=jnp.int32) // TOK)[:, None]
    return (expert_ids * (sources * SLOT) + source * SLOT + position).astype(jnp.int32)


def backward_step(acts, grad_in, expert_ids, probs, w_gate, w_up, w_down):
    tokens_all = acts.shape[0]
    sources = tokens_all // TOK
    total = EXPERTS * sources * SLOT
    flat = slot_layout(expert_ids).reshape(-1)
    token_of_pair = jnp.repeat(jnp.arange(tokens_all, dtype=jnp.int32), TOPK)
    owner = jnp.full((total,), tokens_all, jnp.int32).at[flat].set(token_of_pair)
    weight = jnp.zeros((total,), jnp.float32).at[flat].set(probs.reshape(-1).astype(jnp.float32))
    padded_acts = jnp.concatenate([acts, jnp.zeros((1, D), acts.dtype)], 0)
    padded_grad = jnp.concatenate([grad_in, jnp.zeros((1, D), grad_in.dtype)], 0)
    input_rows = padded_acts[owner].reshape(EXPERTS, sources * SLOT, D)
    grad_rows = (padded_grad[owner].astype(jnp.float32) * weight[:, None]).astype(jnp.bfloat16)
    grad_rows = grad_rows.reshape(EXPERTS, sources * SLOT, D)
    rows_wide = input_rows.astype(jnp.float32)
    gate_wide = w_gate.astype(jnp.float32)
    up_wide = w_up.astype(jnp.float32)
    gate_pre = jnp.einsum("erd,edf->erf", rows_wide, gate_wide)
    up_pre = jnp.einsum("erd,edf->erf", rows_wide, up_wide)
    sigma = jax.nn.sigmoid(gate_pre)
    active = gate_pre * sigma
    hidden = (active * up_pre).astype(jnp.bfloat16)
    grads_wide = grad_rows.astype(jnp.float32)
    hidden_grad = jnp.einsum("erd,efd->erf", grads_wide, w_down.astype(jnp.float32))
    gate_grad = (hidden_grad * up_pre * sigma * (1.0 + gate_pre * (1.0 - sigma))).astype(jnp.bfloat16)
    up_grad = (hidden_grad * active).astype(jnp.bfloat16)
    row_grad = jnp.einsum("erf,edf->erd", gate_grad.astype(jnp.float32), gate_wide)
    row_grad = row_grad + jnp.einsum("erf,edf->erd", up_grad.astype(jnp.float32), up_wide)
    row_grad = row_grad.astype(jnp.bfloat16)
    down_term = jnp.einsum("erf,erd->efd", hidden.astype(jnp.float32), grads_wide)
    gathered = row_grad.reshape(total, D)[flat].reshape(tokens_all, TOPK, D).astype(jnp.float32)
    result = (grad_in.astype(jnp.float32) + jnp.sum(gathered, axis=1)).astype(jnp.bfloat16)
    return result, down_term


def section_pass(incoming, acts, expert_ids, probs, w_gate, w_up, w_down):
    results = []
    down_sum = jnp.zeros((EXPERTS, FF, D), jnp.float32)
    for moment in range(TICKS):
        result, term = backward_step(acts[moment], incoming[moment], expert_ids[moment], probs[moment], w_gate, w_up, w_down)
        results.append(result)
        down_sum = down_sum + term
    return jnp.stack(results, axis=0), down_sum.astype(jnp.bfloat16)


def reference(acts, carried, loss_grad, expert_ids, probs, w_gate, w_up, w_down):
    last = acts.shape[0] - 1
    top_out, top_down = section_pass(loss_grad, acts[last], expert_ids[last], probs[last], w_gate[last], w_up[last], w_down[last])

    def step_down(above, pieces):
        carried_one, acts_one, ids_one, probs_one, gate_one, up_one, down_one = pieces
        incoming = jnp.concatenate([carried_one[None], above[:-1]], 0)
        result, down_one_grad = section_pass(incoming, acts_one, ids_one, probs_one, gate_one, up_one, down_one)
        return result, (result, down_one_grad)

    unused, stacked = lax.scan(step_down, top_out, (carried[:-1], acts[:-1], expert_ids[:-1], probs[:-1], w_gate[:-1], w_up[:-1], w_down[:-1]), reverse=True)
    rest_out, rest_down = stacked
    out_grad = jnp.concatenate([rest_out, top_out[None]], 0)
    down_grad = jnp.concatenate([rest_down, top_down[None]], 0)
    return out_grad, down_grad
```

```python
import jax
import jax.numpy as jnp
from jax import lax
from jax.sharding import PartitionSpec as P


def passed_along(value, axis, steps):
    count = lax.axis_size(axis)
    leading, last = (max(0, -steps), min(count, count - steps))
    return lax.ppermute(value, axis, [(source, source + steps) for source in range(leading, last)])


def per_device(acts, carried, loss_grad, expert_ids, probs, w_gate, w_up, w_down):
    experts = lax.axis_size("expert")
    ticks, tokens, width = acts.shape[1:]
    gate_weight, up_weight, down_weight = w_gate[0, 0], w_up[0, 0], w_down[0, 0]
    is_last = lax.axis_index("section") == lax.axis_size("section") - 1
    me = lax.axis_index("expert")
    hit = expert_ids[0][..., None] == jnp.arange(experts, dtype=jnp.int32)
    routed = jnp.sum(jnp.where(hit, probs[0][..., None], 0.0), axis=2)
    routed = lax.all_gather(routed, "expert", axis=1, tiled=True)
    mine = jnp.arange(experts, dtype=jnp.int32) == me
    weight = jnp.sum(jnp.where(mine, routed, 0.0), axis=2)
    contract = (((1,), (1,)), ((), ()))
    rows_contract = (((0,), (0,)), ((), ()))
    incoming = jnp.where(is_last, loss_grad[0], carried[0])
    rows = lax.all_gather(acts[0], "expert", axis=1, tiled=True)
    results = []
    down_sum = jnp.zeros(down_weight.shape, jnp.float32)
    for moment in range(ticks):
        gate_pre = jnp.dot(rows[moment], gate_weight, preferred_element_type=jnp.float32)
        up_pre = jnp.dot(rows[moment], up_weight, preferred_element_type=jnp.float32)
        sigma = jax.nn.sigmoid(gate_pre)
        active = gate_pre * sigma
        hidden = (active * up_pre).astype(jnp.bfloat16)
        gathered = lax.all_gather(incoming, "expert", axis=0, tiled=True)
        grad = (gathered.astype(jnp.float32) * weight[moment][:, None]).astype(jnp.bfloat16)
        hidden_grad = lax.dot_general(grad, down_weight, contract, preferred_element_type=jnp.float32)
        gate_grad = (hidden_grad * up_pre * sigma * (1.0 + gate_pre * (1.0 - sigma))).astype(jnp.bfloat16)
        up_grad = (hidden_grad * active).astype(jnp.bfloat16)
        row_grad = lax.dot_general(gate_grad, gate_weight, contract, preferred_element_type=jnp.float32)
        row_grad = row_grad + lax.dot_general(up_grad, up_weight, contract, preferred_element_type=jnp.float32)
        back = lax.psum_scatter(row_grad.astype(jnp.bfloat16), "expert", scatter_dimension=0, tiled=True)
        result = (incoming.astype(jnp.float32) + back.astype(jnp.float32)).astype(jnp.bfloat16)
        results.append(result)
        down_sum = down_sum + lax.dot_general(hidden, grad, rows_contract, preferred_element_type=jnp.float32)
        if moment + 1 < ticks:
            arriving = passed_along(result, "section", -1)
            incoming = jnp.where(is_last, loss_grad[moment + 1], arriving)
    out_grad = jnp.stack(results, axis=0)[None]
    return (out_grad, down_sum.astype(jnp.bfloat16)[None, None])


def solution(mesh):
    return jax.shard_map(
        per_device,
        mesh=mesh,
        in_specs=(
            P("section", None, "expert", None),
            P("section", "expert", None),
            P(None, "expert", None),
            P("section", None, "expert", None),
            P("section", None, "expert", None),
            P("section", "expert", None, None),
            P("section", "expert", None, None),
            P("section", "expert", None, None),
        ),
        out_specs=(P("section", None, "expert", None), P("section", "expert", None, None)),
        check_vma=False,
    )
```

```python
import functools

import jax
import jax.numpy as jnp
from jax import lax
from jax.experimental import pallas as pl
from jax.experimental.pallas import tpu as pltpu
from jax.sharding import PartitionSpec as P

MESH = pl.DeviceIdType.MESH
BF16 = jnp.bfloat16
F32 = jnp.float32


def kernel(
    sections, lines,
    acts_ref, carried_ref, loss_ref, routed_ref, gate_ref, up_ref, down_ref,
    out_ref, down_out_ref,
    acts_all, inc_all, routed_all, wide, wide_t, down_t, chosen, columns,
    steep, active_buf, hidden_buf, grad_buf, total,
    part, core_in, x_out, x_in, z_out, z_in, own_sum,
    ag_send, ag_recv, rs_send, rs_recv, relay_send, relay_recv,
):
    ticks, tokens, width = acts_ref.shape
    ff = gate_ref.shape[1]
    section = lax.axis_index("section")
    me = lax.axis_index("expert")
    a = me // 4
    b = lax.rem(me // 2, 2)
    c = lax.rem(me, 2)
    nb, nc = 1 - b, 1 - c
    g = b * 2 + c
    ng = nb * 2 + c
    x_peer = a * 4 + nb * 2 + c
    core_peer = a * 4 + b * 2 + nc
    is_last = section == sections - 1
    half = 2 * lines * tokens

    def line_at(j):
        return lax.rem(a + j, lines)

    def line_peer(j):
        return line_at(j) * 4 + g

    def line_back(j):
        return lax.rem(a + lines - j, lines)

    def rows_of(kind_buf, t):
        return kind_buf if t is None else kind_buf.at[t]

    def gather_copy(buf, t, kind, index, ref_of, target):
        ref = ref_of(rows_of(buf, t))
        return pltpu.make_async_remote_copy(
            src_ref=ref, dst_ref=ref,
            send_sem=ag_send.at[kind, index], recv_sem=ag_recv.at[kind, index],
            device_id={"expert": target}, device_id_type=MESH,
        )

    def z_copy(buf, t, kind, j):
        return gather_copy(buf, t, kind, j - 1, lambda r: r.at[g, a], line_peer(j))

    def x_copy(buf, t, kind, j):
        return gather_copy(buf, t, kind, lines - 1 + j, lambda r: r.at[g, line_back(j)], x_peer)

    def core_copy(buf, t, kind, i):
        group = g if i == 0 else ng
        return gather_copy(buf, t, kind, 2 * lines - 1 + i, lambda r: r.at[group], core_peer)

    def gather_start(buf, t, kind):
        for j in range(1, lines):
            z_copy(buf, t, kind, j).start()
        x_copy(buf, t, kind, 0).start()

    def gather_lines(buf, t, kind):
        for j in range(1, lines):
            z_copy(buf, t, kind, j).wait_recv()
            x_copy(buf, t, kind, j).start()
        core_copy(buf, t, kind, 0).start()

    def gather_cross(buf, t, kind):
        for j in range(lines):
            x_copy(buf, t, kind, j).wait_recv()
        core_copy(buf, t, kind, 1).start()

    def gather_drain(buf, t, kind):
        for j in range(1, lines):
            z_copy(buf, t, kind, j).wait_send()
        for j in range(lines):
            x_copy(buf, t, kind, j).wait_send()
        for i in range(2):
            core_copy(buf, t, kind, i).wait_send()

    def acts_kind(t):
        return 1 + t

    def inc_kind(t):
        return 1 + ticks + t

    def back_copy(t, index, src, dst, target):
        return pltpu.make_async_remote_copy(
            src_ref=src, dst_ref=dst,
            send_sem=rs_send.at[t, index], recv_sem=rs_recv.at[t, index],
            device_id={"expert": target}, device_id_type=MESH,
        )

    def back_core(t, i):
        group = (nb if i == 0 else b) * 2 + nc
        return back_copy(t, i, part.at[t, group], core_in.at[t, i], core_peer)

    def back_x(t, j):
        return back_copy(t, 2 + j, x_out.at[t, line_at(j)], x_in.at[t, line_at(j)], x_peer)

    def back_z(t, j):
        return back_copy(t, 1 + lines + j, z_out.at[t, j - 1], z_in.at[t, j - 1], line_peer(j))

    def relay(t):
        down_one = lax.rem(section + sections - 1, sections)
        return pltpu.make_async_remote_copy(
            src_ref=out_ref.at[t], dst_ref=inc_all.at[t + 1, g, a],
            send_sem=relay_send.at[t], recv_sem=relay_recv.at[t],
            device_id={"section": down_one}, device_id_type=MESH,
        )

    barrier = pltpu.get_barrier_semaphore()
    for j in range(1, lines):
        pl.semaphore_signal(barrier, inc=1, device_id={"expert": line_peer(j)}, device_id_type=MESH)
    for peer in (x_peer, core_peer):
        pl.semaphore_signal(barrier, inc=1, device_id={"expert": peer}, device_id_type=MESH)
    for step in (1, sections - 1):
        other = lax.rem(section + step, sections)
        pl.semaphore_signal(barrier, inc=1, device_id={"section": other}, device_id_type=MESH)

    acts_all[:, g, a] = acts_ref[...]
    routed_all[g, a] = routed_ref[...]

    @pl.when(is_last)
    def _():
        inc_all[:, g, a] = loss_ref[...]

    @pl.when(jnp.logical_not(is_last))
    def _():
        inc_all[0, g, a] = carried_ref[...]

    pl.semaphore_wait(barrier, lines + 3)

    gather_start(routed_all, None, 0)
    gather_start(acts_all, 0, acts_kind(0))
    gather_start(inc_all, 0, inc_kind(0))
    wide[:, :ff] = gate_ref[...]
    wide[:, ff:] = up_ref[...]
    wide_t[:ff, :] = gate_ref[...].T
    wide_t[ff:, :] = up_ref[...].T
    down_t[...] = down_ref[...].T
    total[...] = jnp.zeros_like(total)
    gather_lines(routed_all, None, 0)
    gather_lines(acts_all, 0, acts_kind(0))
    gather_cross(routed_all, None, 0)
    core_copy(routed_all, None, 0, 0).wait_recv()
    core_copy(routed_all, None, 0, 1).wait_recv()
    experts = 4 * lines
    table = routed_all[...].reshape(experts, experts, ticks * tokens)
    mine = lax.broadcasted_iota(jnp.int32, table.shape, 1) == me
    chosen[...] = jnp.sum(jnp.where(mine, table, 0.0), axis=1)
    for i in range(2):
        columns[i] = chosen[pl.ds(i * 2 * lines, 2 * lines), :].T

    def forward(t, side):
        rows = acts_all[t, pl.ds(side * 2, 2)].reshape(half, width)
        pre = jnp.dot(rows, wide[...], preferred_element_type=F32)
        gate_pre, up_pre = pre[:, :ff], pre[:, ff:]
        sigma = 1.0 / (1.0 + jnp.exp(-gate_pre))
        active = gate_pre * sigma
        hidden_buf[side] = (active * up_pre).astype(BF16)
        steep[side] = up_pre * sigma * (1.0 + gate_pre * (1.0 - sigma))
        active_buf[side] = active

    def backward(t, side):
        scale = columns[side, pl.ds(pl.multiple_of(t * tokens, tokens), tokens), :]
        for p in range(2 * lines):
            block = inc_all[t, side * 2 + p // lines, p % lines].astype(F32)
            grad_buf[side, pl.ds(p * tokens, tokens), :] = (block * scale[:, p : p + 1]).astype(BF16)
        hidden_grad = jnp.dot(grad_buf[side], down_t[...], preferred_element_type=F32)
        both = jnp.concatenate(
            [(hidden_grad * steep[side]).astype(BF16), (hidden_grad * active_buf[side]).astype(BF16)], axis=1
        )
        row_grad = jnp.dot(both, wide_t[...], preferred_element_type=F32)
        part[t, pl.ds(side * 2, 2)] = row_grad.astype(BF16).reshape(2, lines, tokens, width)

    def tick(t, carry):
        more = t + 1 < ticks

        @pl.when(t > 0)
        def _():
            @pl.when(jnp.logical_not(is_last))
            def _():
                relay(t - 1).wait_recv()

            gather_start(inc_all, t, inc_kind(t))

        gather_cross(acts_all, t, acts_kind(t))
        core_copy(acts_all, t, acts_kind(t), 0).wait_recv()
        forward(t, b)
        gather_lines(inc_all, t, inc_kind(t))
        core_copy(acts_all, t, acts_kind(t), 1).wait_recv()
        forward(t, nb)
        core_copy(inc_all, t, inc_kind(t), 0).wait_recv()
        backward(t, b)
        back_core(t, 1).start()
        gather_cross(inc_all, t, inc_kind(t))
        core_copy(inc_all, t, inc_kind(t), 1).wait_recv()

        @pl.when(more)
        def _():
            gather_start(acts_all, t + 1, acts_kind(t + 1))

        backward(t, nb)
        back_core(t, 0).start()
        back_core(t, 0).wait_recv()
        for j in range(lines):
            where = line_at(j)
            pair = part[t, ng, where].astype(F32) + core_in[t, 0, where].astype(F32)
            x_out[t, where] = pair.astype(BF16)
            back_x(t, j).start()

        for i in range(2):
            total[...] += lax.dot_general(
                hidden_buf[i], grad_buf[i], (((0,), (0,)), ((), ())), preferred_element_type=F32
            )

        @pl.when(more)
        def _():
            gather_lines(acts_all, t + 1, acts_kind(t + 1))

        back_core(t, 1).wait_recv()
        for j in list(range(1, lines)) + [0]:
            back_x(t, j).wait_recv()
            where = line_at(j)
            quad = part[t, g, where].astype(F32) + core_in[t, 1, where].astype(F32)
            quad = quad + x_in[t, where].astype(F32)
            if j:
                z_out[t, j - 1] = quad.astype(BF16)
                back_z(t, j).start()
            else:
                own_sum[...] = quad + inc_all[t, g, a].astype(F32)
        result = own_sum[...]
        for j in range(1, lines):
            back_z(t, j).wait_recv()
            result = result + z_in[t, j - 1].astype(F32)
        out_ref[t] = result.astype(BF16)

        @pl.when(jnp.logical_and(more, section > 0))
        def _():
            relay(t).start()

        return carry

    lax.fori_loop(0, ticks, tick, 0)
    down_out_ref[...] = total[...].astype(BF16)
    gather_drain(routed_all, None, 0)

    def drain(t, carry):
        gather_drain(acts_all, t, acts_kind(t))
        gather_drain(inc_all, t, inc_kind(t))
        for i in range(2):
            back_core(t, i).wait_send()
        for j in range(lines):
            back_x(t, j).wait_send()
        for j in range(1, lines):
            back_z(t, j).wait_send()

        @pl.when(jnp.logical_and(t + 1 < ticks, section > 0))
        def _():
            relay(t).wait_send()

        return carry

    lax.fori_loop(0, ticks, drain, 0)


def per_device(acts, carried, loss_grad, expert_ids, probs, w_gate, w_up, w_down):
    sections = lax.axis_size("section")
    experts = lax.axis_size("expert")
    lines = experts // 4
    ticks, tokens, width = acts.shape[1:]
    ff = w_gate.shape[3]
    hit = jnp.arange(experts, dtype=jnp.int32)[:, None, None] == expert_ids.reshape(1, ticks * tokens, -1)
    routed = jnp.sum(jnp.where(hit, probs.reshape(1, ticks * tokens, -1), 0.0), axis=2)
    kinds, hops = 1 + 2 * ticks, 2 * lines + 1
    half = 2 * lines * tokens
    dma = pltpu.SemaphoreType.DMA
    vmem = pltpu.VMEM
    gathered = (ticks, 4, lines, tokens, width)
    out, down = pl.pallas_call(
        functools.partial(kernel, sections, lines),
        out_shape=(
            jax.ShapeDtypeStruct((ticks, tokens, width), BF16),
            jax.ShapeDtypeStruct((ff, width), BF16),
        ),
        in_specs=[pl.BlockSpec(memory_space=vmem)] * 7,
        out_specs=(pl.BlockSpec(memory_space=vmem),) * 2,
        scratch_shapes=[
            vmem(gathered, BF16), vmem(gathered, BF16), vmem((4, lines, experts, ticks * tokens), F32),
            vmem((width, 2 * ff), BF16), vmem((2 * ff, width), BF16), vmem((width, ff), BF16),
            vmem((experts, ticks * tokens), F32), vmem((2, ticks * tokens, 2 * lines), F32),
            vmem((2, half, ff), F32), vmem((2, half, ff), F32), vmem((2, half, ff), BF16),
            vmem((2, half, width), BF16), vmem((ff, width), F32),
            vmem(gathered, BF16), vmem((ticks, 2, lines, tokens, width), BF16),
            vmem((ticks, lines, tokens, width), BF16), vmem((ticks, lines, tokens, width), BF16),
            vmem((ticks, lines - 1, tokens, width), BF16), vmem((ticks, lines - 1, tokens, width), BF16),
            vmem((tokens, width), F32),
            dma((kinds, hops)), dma((kinds, hops)), dma((ticks, 1 + 2 * lines)), dma((ticks, 1 + 2 * lines)),
            dma((ticks,)), dma((ticks,)),
        ],
        compiler_params=pltpu.CompilerParams(
            collective_id=0, has_side_effects=True, vmem_limit_bytes=60 * 1024 * 1024
        ),
        cost_estimate=pl.CostEstimate(
            flops=12 * ticks * experts * tokens * width * ff, bytes_accessed=8 * width * ff, transcendentals=0
        ),
        name="window",
    )(acts[0], carried[0], loss_grad, routed, w_gate[0, 0], w_up[0, 0], w_down[0, 0])
    return out[None], down[None, None]


def solution(mesh):
    return jax.shard_map(
        per_device,
        mesh=mesh,
        in_specs=(
            P("section", None, "expert", None),
            P("section", "expert", None),
            P(None, "expert", None),
            P("section", None, "expert", None),
            P("section", None, "expert", None),
            P("section", "expert", None, None),
            P("section", "expert", None, None),
            P("section", "expert", None, None),
        ),
        out_specs=(P("section", None, "expert", None), P("section", "expert", None, None)),
        check_vma=False,
    )
```

```python
import functools

import jax
import jax.numpy as jnp
from jax import lax
from jax.experimental import pallas as pl
from jax.experimental.pallas import tpu as pltpu
from jax.sharding import PartitionSpec as P

MESH = pl.DeviceIdType.MESH
BF16 = jnp.bfloat16
F32 = jnp.float32
HALVES = 2


def kernel(
    sections, lines,
    acts_ref, carried_ref, loss_ref, routed_ref, gate_ref, up_ref, down_ref,
    out_ref, down_out_ref,
    acts_all, inc_all, routed_all, wide, wide_t, down_t, columns,
    steep, active_buf, hidden_buf, grad_buf, total,
    part, core_in, x_out, x_in, z_out, z_in, own_sum,
    ag_send, ag_recv, rs_send, rs_recv, relay_send, relay_recv,
):
    units, tokens, width = acts_ref.shape
    halves = carried_ref.shape[0]
    experts = 4 * lines
    count = experts * tokens
    ff = gate_ref.shape[1]
    section = lax.axis_index("section")
    me = lax.axis_index("expert")
    a = me // 4
    b = lax.rem(me // 2, 2)
    c = lax.rem(me, 2)
    nb, nc = 1 - b, 1 - c
    g = b * 2 + c
    ng = nb * 2 + c
    x_peer = a * 4 + nb * 2 + c
    core_peer = a * 4 + b * 2 + nc
    is_last = section == sections - 1

    def line_at(j):
        return lax.rem(a + j, lines)

    def line_peer(j):
        return line_at(j) * 4 + g

    def line_back(j):
        return lax.rem(a + lines - j, lines)

    def rows_of(kind_buf, t):
        return kind_buf if t is None else kind_buf.at[t]

    def gather_copy(buf, t, kind, index, ref_of, target):
        ref = ref_of(rows_of(buf, t))
        return pltpu.make_async_remote_copy(
            src_ref=ref, dst_ref=ref,
            send_sem=ag_send.at[kind, index], recv_sem=ag_recv.at[kind, index],
            device_id={"expert": target}, device_id_type=MESH,
        )

    def z_copy(buf, t, kind, j):
        return gather_copy(buf, t, kind, j - 1, lambda r: r.at[g, a], line_peer(j))

    def x_copy(buf, t, kind, j):
        return gather_copy(buf, t, kind, lines - 1 + j, lambda r: r.at[g, line_back(j)], x_peer)

    def core_copy(buf, t, kind, i):
        group = g if i == 0 else ng
        return gather_copy(buf, t, kind, 2 * lines - 1 + i, lambda r: r.at[group], core_peer)

    def gather_start(buf, t, kind):
        for j in range(1, lines):
            z_copy(buf, t, kind, j).start()
        x_copy(buf, t, kind, 0).start()

    def gather_lines(buf, t, kind):
        for j in range(1, lines):
            z_copy(buf, t, kind, j).wait_recv()
            x_copy(buf, t, kind, j).start()
        core_copy(buf, t, kind, 0).start()

    def gather_cross(buf, t, kind):
        for j in range(lines):
            x_copy(buf, t, kind, j).wait_recv()
        core_copy(buf, t, kind, 1).start()

    def gather_drain(buf, t, kind):
        for j in range(1, lines):
            z_copy(buf, t, kind, j).wait_send()
        for j in range(lines):
            x_copy(buf, t, kind, j).wait_send()
        for i in range(2):
            core_copy(buf, t, kind, i).wait_send()

    def acts_kind(t):
        return 1 + t

    def inc_kind(t):
        return 1 + units + t

    def back_copy(t, index, src, dst, target):
        return pltpu.make_async_remote_copy(
            src_ref=src, dst_ref=dst,
            send_sem=rs_send.at[t, index], recv_sem=rs_recv.at[t, index],
            device_id={"expert": target}, device_id_type=MESH,
        )

    def back_core(t, i):
        group = (nb if i == 0 else b) * 2 + nc
        return back_copy(t, i, part.at[t, group], core_in.at[t, i], core_peer)

    def back_x(t, j):
        return back_copy(t, 2 + j, x_out.at[t, line_at(j)], x_in.at[t, line_at(j)], x_peer)

    def back_z(t, j):
        return back_copy(t, 1 + lines + j, z_out.at[t, j - 1], z_in.at[t, j - 1], line_peer(j))

    def relay(t):
        down_one = lax.rem(section + sections - 1, sections)
        return pltpu.make_async_remote_copy(
            src_ref=out_ref.at[t], dst_ref=inc_all.at[t + halves, g, a],
            send_sem=relay_send.at[t], recv_sem=relay_recv.at[t],
            device_id={"section": down_one}, device_id_type=MESH,
        )

    barrier = pltpu.get_barrier_semaphore()
    for j in range(1, lines):
        pl.semaphore_signal(barrier, inc=1, device_id={"expert": line_peer(j)}, device_id_type=MESH)
    for peer in (x_peer, core_peer):
        pl.semaphore_signal(barrier, inc=1, device_id={"expert": peer}, device_id_type=MESH)
    for step in (1, sections - 1):
        other = lax.rem(section + step, sections)
        pl.semaphore_signal(barrier, inc=1, device_id={"section": other}, device_id_type=MESH)

    acts_all[:, g, a] = acts_ref[...]
    routed_all[g, a] = routed_ref[...]

    @pl.when(is_last)
    def _():
        inc_all[:, g, a] = loss_ref[...]

    @pl.when(jnp.logical_not(is_last))
    def _():
        inc_all[:halves, g, a] = carried_ref[...]

    pl.semaphore_wait(barrier, lines + 3)

    def forward(u):
        rows = acts_all[u].reshape(count, width)
        pre = jnp.dot(rows, wide[...], preferred_element_type=F32)
        gate_pre, up_pre = pre[:, :ff], pre[:, ff:]
        sigma = 1.0 / (1.0 + jnp.exp(-gate_pre))
        active = gate_pre * sigma
        hidden_buf[...] = (active * up_pre).astype(BF16)
        steep[...] = up_pre * sigma * (1.0 + gate_pre * (1.0 - sigma))
        active_buf[...] = active

    def backward(u):
        scale = columns[pl.ds(pl.multiple_of(u * tokens, tokens), tokens), :]
        for p in range(experts):
            block = inc_all[u, p // lines, p % lines].astype(F32)
            grad_buf[pl.ds(p * tokens, tokens), :] = (block * scale[:, p : p + 1]).astype(BF16)
        hidden_grad = jnp.dot(grad_buf[...], down_t[...], preferred_element_type=F32)
        both = jnp.concatenate(
            [(hidden_grad * steep[...]).astype(BF16), (hidden_grad * active_buf[...]).astype(BF16)], axis=1
        )
        row_grad = jnp.dot(both, wide_t[...], preferred_element_type=F32)
        part[u] = row_grad.astype(BF16).reshape(4, lines, tokens, width)

    def core_arrived(buf, u, kind):
        for i in range(2):
            core_copy(buf, u, kind, i).wait_recv()

    gather_start(routed_all, None, 0)
    gather_start(acts_all, 0, acts_kind(0))
    gather_start(inc_all, 0, inc_kind(0))
    gather_start(acts_all, 1, acts_kind(1))
    wide[:, :ff] = gate_ref[...]
    wide[:, ff:] = up_ref[...]
    wide_t[:ff, :] = gate_ref[...].T
    wide_t[ff:, :] = up_ref[...].T
    down_t[...] = down_ref[...].T
    total[...] = jnp.zeros_like(total)
    gather_lines(routed_all, None, 0)
    gather_lines(acts_all, 0, acts_kind(0))
    gather_lines(inc_all, 0, inc_kind(0))
    gather_cross(routed_all, None, 0)
    gather_cross(acts_all, 0, acts_kind(0))
    gather_lines(acts_all, 1, acts_kind(1))
    core_arrived(routed_all, None, 0)
    table = routed_all[...].reshape(experts, experts, units * tokens)
    mine = lax.broadcasted_iota(jnp.int32, table.shape, 1) == me
    columns[...] = jnp.sum(jnp.where(mine, table, 0.0), axis=1).T
    core_arrived(acts_all, 0, acts_kind(0))
    forward(0)
    gather_cross(inc_all, 0, inc_kind(0))
    core_arrived(inc_all, 0, inc_kind(0))

    def step(u, carry):
        more = u + 1 < units
        more_two = u + 2 < units
        backward(u)
        back_core(u, 0).start()
        back_core(u, 1).start()

        @pl.when(more)
        def _():
            @pl.when(jnp.logical_and(u + 1 >= halves, jnp.logical_not(is_last)))
            def _():
                relay(u + 1 - halves).wait_recv()

            gather_start(inc_all, u + 1, inc_kind(u + 1))

        back_core(u, 0).wait_recv()
        for j in range(lines):
            where = line_at(j)
            pair = part[u, ng, where].astype(F32) + core_in[u, 0, where].astype(F32)
            x_out[u, where] = pair.astype(BF16)
            back_x(u, j).start()

        @pl.when(more)
        def _():
            gather_cross(acts_all, u + 1, acts_kind(u + 1))

        @pl.when(more_two)
        def _():
            gather_start(acts_all, u + 2, acts_kind(u + 2))

        total[...] += lax.dot_general(
            hidden_buf[...], grad_buf[...], (((0,), (0,)), ((), ())), preferred_element_type=F32
        )

        @pl.when(more)
        def _():
            gather_lines(inc_all, u + 1, inc_kind(u + 1))
            core_arrived(acts_all, u + 1, acts_kind(u + 1))
            forward(u + 1)

        back_core(u, 1).wait_recv()
        for j in list(range(1, lines)) + [0]:
            back_x(u, j).wait_recv()
            where = line_at(j)
            quad = part[u, g, where].astype(F32) + core_in[u, 1, where].astype(F32)
            quad = quad + x_in[u, where].astype(F32)
            if j:
                z_out[u, j - 1] = quad.astype(BF16)
                back_z(u, j).start()
            else:
                own_sum[...] = quad + inc_all[u, g, a].astype(F32)

        @pl.when(more_two)
        def _():
            gather_lines(acts_all, u + 2, acts_kind(u + 2))

        @pl.when(more)
        def _():
            gather_cross(inc_all, u + 1, inc_kind(u + 1))

        result = own_sum[...]
        for j in range(1, lines):
            back_z(u, j).wait_recv()
            result = result + z_in[u, j - 1].astype(F32)
        out_ref[u] = result.astype(BF16)

        @pl.when(jnp.logical_and(u + halves < units, section > 0))
        def _():
            relay(u).start()

        @pl.when(more)
        def _():
            core_arrived(inc_all, u + 1, inc_kind(u + 1))

        return carry

    lax.fori_loop(0, units, step, 0)
    down_out_ref[...] = total[...].astype(BF16)
    gather_drain(routed_all, None, 0)

    def drain(u, carry):
        gather_drain(acts_all, u, acts_kind(u))
        gather_drain(inc_all, u, inc_kind(u))
        for i in range(2):
            back_core(u, i).wait_send()
        for j in range(lines):
            back_x(u, j).wait_send()
        for j in range(1, lines):
            back_z(u, j).wait_send()

        @pl.when(jnp.logical_and(u + halves < units, section > 0))
        def _():
            relay(u).wait_send()

        return carry

    lax.fori_loop(0, units, drain, 0)


def per_device(acts, carried, loss_grad, expert_ids, probs, w_gate, w_up, w_down):
    sections = lax.axis_size("section")
    experts = lax.axis_size("expert")
    lines = experts // 4
    ticks, tokens, width = acts.shape[1:]
    ff = w_gate.shape[3]
    hit = jnp.arange(experts, dtype=jnp.int32)[:, None, None] == expert_ids.reshape(1, ticks * tokens, -1)
    routed = jnp.sum(jnp.where(hit, probs.reshape(1, ticks * tokens, -1), 0.0), axis=2)
    halves = HALVES if tokens % (16 * HALVES) == 0 else 1
    units, rows = ticks * halves, tokens // halves
    kinds, hops = 1 + 2 * units, 2 * lines + 1
    count = experts * rows
    dma = pltpu.SemaphoreType.DMA
    vmem = pltpu.VMEM
    gathered = (units, 4, lines, rows, width)
    out, down = pl.pallas_call(
        functools.partial(kernel, sections, lines),
        out_shape=(
            jax.ShapeDtypeStruct((units, rows, width), BF16),
            jax.ShapeDtypeStruct((ff, width), BF16),
        ),
        in_specs=[pl.BlockSpec(memory_space=vmem)] * 7,
        out_specs=(pl.BlockSpec(memory_space=vmem),) * 2,
        scratch_shapes=[
            vmem(gathered, BF16), vmem(gathered, BF16), vmem((4, lines, experts, ticks * tokens), F32),
            vmem((width, 2 * ff), BF16), vmem((2 * ff, width), BF16), vmem((width, ff), BF16),
            vmem((ticks * tokens, experts), F32),
            vmem((count, ff), F32), vmem((count, ff), F32), vmem((count, ff), BF16),
            vmem((count, width), BF16), vmem((ff, width), F32),
            vmem(gathered, BF16), vmem((units, 2, lines, rows, width), BF16),
            vmem((units, lines, rows, width), BF16), vmem((units, lines, rows, width), BF16),
            vmem((units, lines - 1, rows, width), BF16), vmem((units, lines - 1, rows, width), BF16),
            vmem((rows, width), F32),
            dma((kinds, hops)), dma((kinds, hops)), dma((units, 1 + 2 * lines)), dma((units, 1 + 2 * lines)),
            dma((units,)), dma((units,)),
        ],
        compiler_params=pltpu.CompilerParams(
            collective_id=0, has_side_effects=True, vmem_limit_bytes=60 * 1024 * 1024
        ),
        cost_estimate=pl.CostEstimate(
            flops=12 * ticks * experts * tokens * width * ff, bytes_accessed=8 * width * ff, transcendentals=0
        ),
        name="window",
    )(
        acts.reshape(units, rows, width), carried.reshape(halves, rows, width),
        loss_grad.reshape(units, rows, width), routed, w_gate[0, 0], w_up[0, 0], w_down[0, 0],
    )
    return out.reshape(1, ticks, tokens, width), down[None, None]


def solution(mesh):
    return jax.shard_map(
        per_device,
        mesh=mesh,
        in_specs=(
            P("section", None, "expert", None),
            P("section", "expert", None),
            P(None, "expert", None),
            P("section", None, "expert", None),
            P("section", None, "expert", None),
            P("section", "expert", None, None),
            P("section", "expert", None, None),
            P("section", "expert", None, None),
        ),
        out_specs=(P("section", None, "expert", None), P("section", "expert", None, None)),
        check_vma=False,
    )
```

```python
import functools

import jax
import jax.numpy as jnp
from jax import lax
from jax.experimental import pallas as pl
from jax.experimental.pallas import tpu as pltpu
from jax.sharding import PartitionSpec as P

MESH = pl.DeviceIdType.MESH
BF16 = jnp.bfloat16
F32 = jnp.float32
HALVES = 2


def kernel(
    sections, lines,
    acts_ref, carried_ref, loss_ref, routed_ref, gate_ref, up_ref, down_ref,
    out_ref, down_out_ref,
    acts_all, inc_all, routed_all, gate_in, up_in, down_in, wide, wide_t, down_t, columns,
    steep, active_buf, hidden_buf, total, total_out, total_in,
    part, x_in, z_out, z_in, own_sum,
    ag_send, ag_recv, rs_send, rs_recv, relay_send, relay_recv, pair_send, pair_recv,
):
    units, tokens, width = acts_ref.shape
    halves = carried_ref.shape[0]
    blocks = 2 * lines
    count = blocks * tokens
    ff = gate_ref.shape[1]
    section = lax.axis_index("section")
    me = lax.axis_index("expert")
    a = me // 4
    b = lax.rem(me // 2, 2)
    c = lax.rem(me, 2)
    nb = 1 - b
    x_peer = a * 4 + nb * 2 + c
    core_peer = a * 4 + b * 2 + 1 - c
    is_last = section == sections - 1

    def line_at(j):
        return lax.rem(a + j, lines)

    def line_peer(j):
        return line_at(j) * 4 + b * 2 + c

    def line_back(j):
        return lax.rem(a + lines - j, lines)

    def gather_copy(buf, u, kind, index, where, target):
        ref = buf.at[b, where] if u is None else buf.at[u, b, where]
        return pltpu.make_async_remote_copy(
            src_ref=ref, dst_ref=ref,
            send_sem=ag_send.at[kind, index], recv_sem=ag_recv.at[kind, index],
            device_id={"expert": target}, device_id_type=MESH,
        )

    def z_copy(buf, u, kind, j):
        return gather_copy(buf, u, kind, j - 1, a, line_peer(j))

    def x_copy(buf, u, kind, j):
        return gather_copy(buf, u, kind, lines - 1 + j, line_back(j), x_peer)

    def gather_start(buf, u, kind):
        for j in range(1, lines):
            z_copy(buf, u, kind, j).start()
        x_copy(buf, u, kind, 0).start()

    def gather_lines(buf, u, kind):
        for j in range(1, lines):
            z_copy(buf, u, kind, j).wait_recv()
            x_copy(buf, u, kind, j).start()

    def gather_cross(buf, u, kind):
        for j in range(lines):
            x_copy(buf, u, kind, j).wait_recv()

    def gather_drain(buf, u, kind):
        for j in range(1, lines):
            z_copy(buf, u, kind, j).wait_send()
        for j in range(lines):
            x_copy(buf, u, kind, j).wait_send()

    def acts_kind(u):
        return 1 + u

    def inc_kind(u):
        return 1 + units + u

    def back_copy(u, index, src, dst, target):
        return pltpu.make_async_remote_copy(
            src_ref=src, dst_ref=dst,
            send_sem=rs_send.at[u, index], recv_sem=rs_recv.at[u, index],
            device_id={"expert": target}, device_id_type=MESH,
        )

    def back_x(u, j):
        return back_copy(u, j, part.at[u, nb, line_at(j)], x_in.at[u, line_at(j)], x_peer)

    def back_z(u, j):
        return back_copy(u, lines - 1 + j, z_out.at[u, j - 1], z_in.at[u, j - 1], line_peer(j))

    def relay(u):
        down_one = lax.rem(section + sections - 1, sections)
        return pltpu.make_async_remote_copy(
            src_ref=out_ref.at[u], dst_ref=inc_all.at[u + halves, b, a],
            send_sem=relay_send.at[u], recv_sem=relay_recv.at[u],
            device_id={"section": down_one}, device_id_type=MESH,
        )

    def pair_copy(index, src, dst):
        return pltpu.make_async_remote_copy(
            src_ref=src, dst_ref=dst, send_sem=pair_send.at[index], recv_sem=pair_recv.at[index],
            device_id={"expert": core_peer}, device_id_type=MESH,
        )

    swaps = [
        pair_copy(0, gate_ref, gate_in), pair_copy(1, up_ref, up_in),
        pair_copy(2, down_ref, down_in), pair_copy(3, total_out, total_in),
    ]

    barrier = pltpu.get_barrier_semaphore()
    for j in range(1, lines):
        pl.semaphore_signal(barrier, inc=1, device_id={"expert": line_peer(j)}, device_id_type=MESH)
    for peer in (x_peer, core_peer):
        pl.semaphore_signal(barrier, inc=1, device_id={"expert": peer}, device_id_type=MESH)
    for step in (1, sections - 1):
        other = lax.rem(section + step, sections)
        pl.semaphore_signal(barrier, inc=1, device_id={"section": other}, device_id_type=MESH)

    acts_all[:, b, a] = acts_ref[...]
    routed_all[b, a] = routed_ref[...]

    @pl.when(is_last)
    def _():
        inc_all[:, b, a] = loss_ref[...]

    @pl.when(jnp.logical_not(is_last))
    def _():
        inc_all[:halves, b, a] = carried_ref[...]

    pl.semaphore_wait(barrier, lines + 3)

    def forward(u):
        start = pl.multiple_of(u * tokens, tokens)
        scales = []
        for i in range(2):
            table = columns[i, pl.ds(start, tokens), :]
            column = jnp.concatenate([table[:, p : p + 1] for p in range(blocks)], axis=0)
            scales.append(jnp.broadcast_to(column, (count, ff)))
        scale = jnp.concatenate(scales, axis=1)
        rows = acts_all[u].reshape(count, width)
        pre = jnp.dot(rows, wide[...], preferred_element_type=F32)
        gate_pre, up_pre = pre[:, : 2 * ff], pre[:, 2 * ff :]
        sigma = 1.0 / (1.0 + jnp.exp(-gate_pre))
        active = gate_pre * sigma
        hidden_buf[...] = (active * up_pre * scale).astype(BF16)
        steep[...] = up_pre * sigma * (1.0 + gate_pre * (1.0 - sigma)) * scale
        active_buf[...] = active * scale

    def backward(u):
        rows = inc_all[u].reshape(count, width)
        hidden_grad = jnp.dot(rows, down_t[...], preferred_element_type=F32)
        both = jnp.concatenate(
            [(hidden_grad * steep[...]).astype(BF16), (hidden_grad * active_buf[...]).astype(BF16)], axis=1
        )
        row_grad = jnp.dot(both, wide_t[...], preferred_element_type=F32)
        part[u] = row_grad.astype(BF16).reshape(2, lines, tokens, width)

    gather_start(routed_all, None, 0)
    gather_start(acts_all, 0, acts_kind(0))
    for swap in swaps[:3]:
        swap.start()
    gather_start(inc_all, 0, inc_kind(0))
    gather_start(acts_all, 1, acts_kind(1))
    wide[:, :ff] = gate_ref[...]
    wide[:, 2 * ff : 3 * ff] = up_ref[...]
    gather_lines(routed_all, None, 0)
    gather_lines(acts_all, 0, acts_kind(0))
    gather_lines(inc_all, 0, inc_kind(0))
    wide_t[:ff, :] = gate_ref[...].T
    wide_t[2 * ff : 3 * ff, :] = up_ref[...].T
    down_t[:, :ff] = down_ref[...].T
    gather_lines(acts_all, 1, acts_kind(1))
    total[...] = jnp.zeros_like(total)
    gather_cross(routed_all, None, 0)
    experts = 4 * lines
    table = routed_all[...].reshape(blocks, experts, units * tokens)
    names = lax.broadcasted_iota(jnp.int32, table.shape, 1)
    columns[0] = jnp.sum(jnp.where(names == me, table, 0.0), axis=1).T
    columns[1] = jnp.sum(jnp.where(names == core_peer, table, 0.0), axis=1).T
    swaps[0].wait_recv()
    wide[:, ff : 2 * ff] = gate_in[...]
    wide_t[ff : 2 * ff, :] = gate_in[...].T
    swaps[1].wait_recv()
    wide[:, 3 * ff :] = up_in[...]
    wide_t[3 * ff :, :] = up_in[...].T
    gather_cross(acts_all, 0, acts_kind(0))
    forward(0)
    swaps[2].wait_recv()
    down_t[:, ff:] = down_in[...].T
    gather_cross(inc_all, 0, inc_kind(0))

    def step(u, carry):
        more = u + 1 < units
        more_two = u + 2 < units
        backward(u)
        for j in range(lines):
            back_x(u, j).start()

        @pl.when(more)
        def _():
            @pl.when(jnp.logical_and(u + 1 >= halves, jnp.logical_not(is_last)))
            def _():
                relay(u + 1 - halves).wait_recv()

            gather_start(inc_all, u + 1, inc_kind(u + 1))

        @pl.when(more_two)
        def _():
            gather_start(acts_all, u + 2, acts_kind(u + 2))

        total[...] += lax.dot_general(
            hidden_buf[...], inc_all[u].reshape(count, width), (((0,), (0,)), ((), ())),
            preferred_element_type=F32,
        )

        @pl.when(more)
        def _():
            gather_cross(acts_all, u + 1, acts_kind(u + 1))
            forward(u + 1)
            gather_lines(inc_all, u + 1, inc_kind(u + 1))

        for j in list(range(1, lines)) + [0]:
            back_x(u, j).wait_recv()
            where = line_at(j)
            quad = part[u, b, where].astype(F32) + x_in[u, where].astype(F32)
            if j:
                z_out[u, j - 1] = quad.astype(BF16)
                back_z(u, j).start()
            else:
                own_sum[...] = quad + inc_all[u, b, a].astype(F32)

        @pl.when(more_two)
        def _():
            gather_lines(acts_all, u + 2, acts_kind(u + 2))

        @pl.when(jnp.logical_not(more))
        def _():
            total_out[...] = total[ff:, :].astype(BF16)
            swaps[3].start()

        result = own_sum[...]
        for j in range(1, lines):
            back_z(u, j).wait_recv()
            result = result + z_in[u, j - 1].astype(F32)
        out_ref[u] = result.astype(BF16)

        @pl.when(jnp.logical_and(u + halves < units, section > 0))
        def _():
            relay(u).start()

        @pl.when(more)
        def _():
            gather_cross(inc_all, u + 1, inc_kind(u + 1))

        return carry

    lax.fori_loop(0, units, step, 0)
    swaps[3].wait_recv()
    down_out_ref[...] = (total[:ff, :] + total_in[...].astype(F32)).astype(BF16)
    gather_drain(routed_all, None, 0)
    for swap in swaps:
        swap.wait_send()

    def drain(u, carry):
        gather_drain(acts_all, u, acts_kind(u))
        gather_drain(inc_all, u, inc_kind(u))
        for j in range(lines):
            back_x(u, j).wait_send()
        for j in range(1, lines):
            back_z(u, j).wait_send()

        @pl.when(jnp.logical_and(u + halves < units, section > 0))
        def _():
            relay(u).wait_send()

        return carry

    lax.fori_loop(0, units, drain, 0)


def per_device(acts, carried, loss_grad, expert_ids, probs, w_gate, w_up, w_down):
    sections = lax.axis_size("section")
    experts = lax.axis_size("expert")
    lines = experts // 4
    ticks, tokens, width = acts.shape[1:]
    ff = w_gate.shape[3]
    hit = jnp.arange(experts, dtype=jnp.int32)[:, None, None] == expert_ids.reshape(1, ticks * tokens, -1)
    routed = jnp.sum(jnp.where(hit, probs.reshape(1, ticks * tokens, -1), 0.0), axis=2)
    halves = HALVES
    units, rows = ticks * halves, tokens // halves
    kinds, hops = 1 + 2 * units, 2 * lines - 1
    count = 2 * lines * rows
    dma = pltpu.SemaphoreType.DMA
    vmem = pltpu.VMEM
    gathered = (units, 2, lines, rows, width)
    out, down = pl.pallas_call(
        functools.partial(kernel, sections, lines),
        out_shape=(
            jax.ShapeDtypeStruct((units, rows, width), BF16),
            jax.ShapeDtypeStruct((ff, width), BF16),
        ),
        in_specs=[pl.BlockSpec(memory_space=vmem)] * 7,
        out_specs=(pl.BlockSpec(memory_space=vmem),) * 2,
        scratch_shapes=[
            vmem(gathered, BF16), vmem(gathered, BF16), vmem((2, lines, experts, ticks * tokens), F32),
            vmem((width, ff), BF16), vmem((width, ff), BF16), vmem((ff, width), BF16),
            vmem((width, 4 * ff), BF16), vmem((4 * ff, width), BF16), vmem((width, 2 * ff), BF16),
            vmem((2, ticks * tokens, 2 * lines), F32),
            vmem((count, 2 * ff), F32), vmem((count, 2 * ff), F32), vmem((count, 2 * ff), BF16),
            vmem((2 * ff, width), F32), vmem((ff, width), BF16), vmem((ff, width), BF16),
            vmem(gathered, BF16), vmem((units, lines, rows, width), BF16),
            vmem((units, lines - 1, rows, width), BF16), vmem((units, lines - 1, rows, width), BF16),
            vmem((rows, width), F32),
            dma((kinds, hops)), dma((kinds, hops)), dma((units, hops)), dma((units, hops)),
            dma((units,)), dma((units,)), dma((4,)), dma((4,)),
        ],
        compiler_params=pltpu.CompilerParams(
            collective_id=0, has_side_effects=True, vmem_limit_bytes=60 * 1024 * 1024
        ),
        cost_estimate=pl.CostEstimate(
            flops=12 * ticks * experts * tokens * width * ff, bytes_accessed=8 * width * ff, transcendentals=0
        ),
        name="window",
    )(
        acts.reshape(units, rows, width), carried.reshape(halves, rows, width),
        loss_grad.reshape(units, rows, width), routed, w_gate[0, 0], w_up[0, 0], w_down[0, 0],
    )
    return out.reshape(1, ticks, tokens, width), down[None, None]


def solution(mesh):
    return jax.shard_map(
        per_device,
        mesh=mesh,
        in_specs=(
            P("section", None, "expert", None),
            P("section", "expert", None),
            P(None, "expert", None),
            P("section", None, "expert", None),
            P("section", None, "expert", None),
            P("section", "expert", None, None),
            P("section", "expert", None, None),
            P("section", "expert", None, None),
        ),
        out_specs=(P("section", None, "expert", None), P("section", "expert", None, None)),
        check_vma=False,
    )
```

```python
import functools

import jax
import jax.numpy as jnp
from jax import lax
from jax.experimental import pallas as pl
from jax.experimental.pallas import tpu as pltpu
from jax.sharding import PartitionSpec as P

MESH = pl.DeviceIdType.MESH
BF16 = jnp.bfloat16
F32 = jnp.float32
HALVES = 2


def kernel(
    sections, lines,
    acts_ref, carried_ref, loss_ref, ids_ref, probs_ref, gate_ref, up_ref, down_ref,
    out_wide, total, total_in,
    out_ref,
    acts_all, inc_all, routed_all, gate_in, up_in, down_in, wide, wide_t, down_t, columns,
    steep, active_buf, hidden_buf, total_out,
    part, x_in, z_out, z_in, own_sum,
    ag_send, ag_recv, rs_send, rs_recv, relay_send, relay_recv, pair_send, pair_recv,
):
    units, tokens, width = acts_ref.shape
    halves = carried_ref.shape[0]
    blocks = 2 * lines
    count = blocks * tokens
    ff = gate_ref.shape[1]
    section = lax.axis_index("section")
    me = lax.axis_index("expert")
    a = me // 4
    b = lax.rem(me // 2, 2)
    c = lax.rem(me, 2)
    nb = 1 - b
    x_peer = a * 4 + nb * 2 + c
    core_peer = a * 4 + b * 2 + 1 - c
    is_last = section == sections - 1

    def line_at(j):
        return lax.rem(a + j, lines)

    def line_peer(j):
        return line_at(j) * 4 + b * 2 + c

    def line_back(j):
        return lax.rem(a + lines - j, lines)

    def gather_copy(buf, u, kind, index, where, target):
        ref = buf.at[b, where] if u is None else buf.at[u, b, where]
        return pltpu.make_async_remote_copy(
            src_ref=ref, dst_ref=ref,
            send_sem=ag_send.at[kind, index], recv_sem=ag_recv.at[kind, index],
            device_id={"expert": target}, device_id_type=MESH,
        )

    def z_copy(buf, u, kind, j):
        return gather_copy(buf, u, kind, j - 1, a, line_peer(j))

    def x_copy(buf, u, kind, j):
        return gather_copy(buf, u, kind, lines - 1 + j, line_back(j), x_peer)

    def gather_start(buf, u, kind):
        for j in range(1, lines):
            z_copy(buf, u, kind, j).start()
        x_copy(buf, u, kind, 0).start()

    def gather_lines(buf, u, kind):
        for j in range(1, lines):
            z_copy(buf, u, kind, j).wait_recv()
            x_copy(buf, u, kind, j).start()

    def gather_cross(buf, u, kind):
        for j in range(lines):
            x_copy(buf, u, kind, j).wait_recv()

    def gather_drain(buf, u, kind):
        for j in range(1, lines):
            z_copy(buf, u, kind, j).wait_send()
        for j in range(lines):
            x_copy(buf, u, kind, j).wait_send()

    def acts_kind(u):
        return 1 + u

    def inc_kind(u):
        return 1 + units + u

    def back_copy(u, index, src, dst, target):
        return pltpu.make_async_remote_copy(
            src_ref=src, dst_ref=dst,
            send_sem=rs_send.at[u, index], recv_sem=rs_recv.at[u, index],
            device_id={"expert": target}, device_id_type=MESH,
        )

    def back_x(u, j):
        return back_copy(u, j, part.at[u, nb, line_at(j)], x_in.at[u, line_at(j)], x_peer)

    def back_z(u, j):
        return back_copy(u, lines - 1 + j, z_out.at[u, j - 1], z_in.at[u, j - 1], line_peer(j))

    def relay(u):
        down_one = lax.rem(section + sections - 1, sections)
        return pltpu.make_async_remote_copy(
            src_ref=out_ref.at[u], dst_ref=inc_all.at[u + halves, b, a],
            send_sem=relay_send.at[u], recv_sem=relay_recv.at[u],
            device_id={"section": down_one}, device_id_type=MESH,
        )

    def pair_copy(index, src, dst):
        return pltpu.make_async_remote_copy(
            src_ref=src, dst_ref=dst, send_sem=pair_send.at[index], recv_sem=pair_recv.at[index],
            device_id={"expert": core_peer}, device_id_type=MESH,
        )

    swaps = [
        pair_copy(0, gate_ref, gate_in), pair_copy(1, up_ref, up_in),
        pair_copy(2, down_ref, down_in), pair_copy(3, total_out, total_in),
    ]

    barrier = pltpu.get_barrier_semaphore()
    for j in range(1, lines):
        pl.semaphore_signal(barrier, inc=1, device_id={"expert": line_peer(j)}, device_id_type=MESH)
    for peer in (x_peer, core_peer):
        pl.semaphore_signal(barrier, inc=1, device_id={"expert": peer}, device_id_type=MESH)
    for step in (1, sections - 1):
        other = lax.rem(section + step, sections)
        pl.semaphore_signal(barrier, inc=1, device_id={"section": other}, device_id_type=MESH)

    acts_all[:, b, a] = acts_ref[...]
    moments = range(ids_ref.shape[0])
    names = jnp.concatenate([ids_ref[t] for t in moments], axis=1)
    odds = jnp.concatenate([probs_ref[t] for t in moments], axis=1)
    expert_row = lax.broadcasted_iota(jnp.int32, (4 * lines, names.shape[1]), 0)
    routed = jnp.zeros(expert_row.shape, F32)
    for k in range(names.shape[0]):
        routed = routed + jnp.where(expert_row == names[k : k + 1, :], odds[k : k + 1, :], 0.0)
    routed_all[b, a] = routed

    @pl.when(is_last)
    def _():
        inc_all[:, b, a] = loss_ref[...]

    @pl.when(jnp.logical_not(is_last))
    def _():
        inc_all[:halves, b, a] = carried_ref[...]

    pl.semaphore_wait(barrier, lines + 3)

    def forward(u):
        start = pl.multiple_of(u * tokens, tokens)
        scales = []
        for i in range(2):
            table = columns[i, pl.ds(start, tokens), :]
            column = jnp.concatenate([table[:, p : p + 1] for p in range(blocks)], axis=0)
            scales.append(jnp.broadcast_to(column, (count, ff)))
        scale = jnp.concatenate(scales, axis=1)
        rows = acts_all[u].reshape(count, width)
        pre = jnp.dot(rows, wide[...], preferred_element_type=F32)
        gate_pre, up_pre = pre[:, : 2 * ff], pre[:, 2 * ff :]
        sigma = 1.0 / (1.0 + jnp.exp(-gate_pre))
        active = gate_pre * sigma
        hidden_buf[...] = (active * up_pre * scale).astype(BF16)
        steep[...] = up_pre * sigma * (1.0 + gate_pre * (1.0 - sigma)) * scale
        active_buf[...] = active * scale

    def backward(u):
        rows = inc_all[u].reshape(count, width)
        hidden_grad = jnp.dot(rows, down_t[...], preferred_element_type=F32)
        both = jnp.concatenate(
            [(hidden_grad * steep[...]).astype(BF16), (hidden_grad * active_buf[...]).astype(BF16)], axis=1
        )
        row_grad = jnp.dot(both, wide_t[...], preferred_element_type=F32)
        part[u] = row_grad.astype(BF16).reshape(2, lines, tokens, width)

    gather_start(routed_all, None, 0)
    gather_start(acts_all, 0, acts_kind(0))
    for swap in swaps[:3]:
        swap.start()
    gather_start(inc_all, 0, inc_kind(0))
    gather_start(acts_all, 1, acts_kind(1))
    wide[:, :ff] = gate_ref[...]
    wide[:, 2 * ff : 3 * ff] = up_ref[...]
    gather_lines(routed_all, None, 0)
    gather_lines(acts_all, 0, acts_kind(0))
    gather_lines(inc_all, 0, inc_kind(0))
    wide_t[:ff, :] = gate_ref[...].T
    wide_t[2 * ff : 3 * ff, :] = up_ref[...].T
    down_t[:, :ff] = down_ref[...].T
    gather_lines(acts_all, 1, acts_kind(1))
    total[...] = jnp.zeros_like(total)
    gather_cross(routed_all, None, 0)
    experts = 4 * lines
    table = routed_all[...].reshape(blocks, experts, units * tokens)
    names = lax.broadcasted_iota(jnp.int32, table.shape, 1)
    columns[0] = jnp.sum(jnp.where(names == me, table, 0.0), axis=1).T
    columns[1] = jnp.sum(jnp.where(names == core_peer, table, 0.0), axis=1).T
    swaps[0].wait_recv()
    wide[:, ff : 2 * ff] = gate_in[...]
    wide_t[ff : 2 * ff, :] = gate_in[...].T
    swaps[1].wait_recv()
    wide[:, 3 * ff :] = up_in[...]
    wide_t[3 * ff :, :] = up_in[...].T
    gather_cross(acts_all, 0, acts_kind(0))
    forward(0)
    swaps[2].wait_recv()
    down_t[:, ff:] = down_in[...].T
    gather_cross(inc_all, 0, inc_kind(0))

    def step(u, carry):
        more = u + 1 < units
        more_two = u + 2 < units
        backward(u)
        for j in range(lines):
            back_x(u, j).start()

        @pl.when(more)
        def _():
            @pl.when(jnp.logical_and(u + 1 >= halves, jnp.logical_not(is_last)))
            def _():
                relay(u + 1 - halves).wait_recv()

            gather_start(inc_all, u + 1, inc_kind(u + 1))

        @pl.when(more_two)
        def _():
            gather_start(acts_all, u + 2, acts_kind(u + 2))

        total[...] += lax.dot_general(
            hidden_buf[...], inc_all[u].reshape(count, width), (((0,), (0,)), ((), ())),
            preferred_element_type=F32,
        )

        @pl.when(more)
        def _():
            gather_cross(acts_all, u + 1, acts_kind(u + 1))
            forward(u + 1)
            gather_lines(inc_all, u + 1, inc_kind(u + 1))

        for j in list(range(1, lines)) + [0]:
            back_x(u, j).wait_recv()
            where = line_at(j)
            quad = part[u, b, where].astype(F32) + x_in[u, where].astype(F32)
            if j:
                z_out[u, j - 1] = quad.astype(BF16)
                back_z(u, j).start()
            else:
                own_sum[...] = quad + inc_all[u, b, a].astype(F32)

        @pl.when(more_two)
        def _():
            gather_lines(acts_all, u + 2, acts_kind(u + 2))

        @pl.when(jnp.logical_not(more))
        def _():
            total_out[...] = total[ff:, :].astype(BF16)
            swaps[3].start()

        result = own_sum[...]
        for j in range(1, lines):
            back_z(u, j).wait_recv()
            result = result + z_in[u, j - 1].astype(F32)
        out_wide[u] = result
        out_ref[u] = result.astype(BF16)

        @pl.when(jnp.logical_and(u + halves < units, section > 0))
        def _():
            relay(u).start()

        @pl.when(more)
        def _():
            gather_cross(inc_all, u + 1, inc_kind(u + 1))

        return carry

    lax.fori_loop(0, units, step, 0)
    swaps[3].wait_recv()
    gather_drain(routed_all, None, 0)
    for swap in swaps:
        swap.wait_send()

    def drain(u, carry):
        gather_drain(acts_all, u, acts_kind(u))
        gather_drain(inc_all, u, inc_kind(u))
        for j in range(lines):
            back_x(u, j).wait_send()
        for j in range(1, lines):
            back_z(u, j).wait_send()

        @pl.when(jnp.logical_and(u + halves < units, section > 0))
        def _():
            relay(u).wait_send()

        return carry

    lax.fori_loop(0, units, drain, 0)


def per_device(acts, carried, loss_grad, expert_ids, probs, w_gate, w_up, w_down):
    sections = lax.axis_size("section")
    experts = lax.axis_size("expert")
    lines = experts // 4
    ticks, tokens, width = acts.shape[1:]
    ff = w_gate.shape[3]
    halves = HALVES
    units, rows = ticks * halves, tokens // halves
    kinds, hops = 1 + 2 * units, 2 * lines - 1
    count = 2 * lines * rows
    dma = pltpu.SemaphoreType.DMA
    vmem = pltpu.VMEM
    gathered = (units, 2, lines, rows, width)
    out, down, other_down = pl.pallas_call(
        functools.partial(kernel, sections, lines),
        out_shape=(
            jax.ShapeDtypeStruct((units, rows, width), F32),
            jax.ShapeDtypeStruct((2 * ff, width), F32),
            jax.ShapeDtypeStruct((ff, width), BF16),
        ),
        in_specs=[pl.BlockSpec(memory_space=vmem)] * 8,
        out_specs=(pl.BlockSpec(memory_space=vmem),) * 3,
        scratch_shapes=[
            vmem((units, rows, width), BF16),
            vmem(gathered, BF16), vmem(gathered, BF16), vmem((2, lines, experts, ticks * tokens), F32),
            vmem((width, ff), BF16), vmem((width, ff), BF16), vmem((ff, width), BF16),
            vmem((width, 4 * ff), BF16), vmem((4 * ff, width), BF16), vmem((width, 2 * ff), BF16),
            vmem((2, ticks * tokens, 2 * lines), F32),
            vmem((count, 2 * ff), F32), vmem((count, 2 * ff), F32), vmem((count, 2 * ff), BF16),
            vmem((ff, width), BF16),
            vmem(gathered, BF16), vmem((units, lines, rows, width), BF16),
            vmem((units, lines - 1, rows, width), BF16), vmem((units, lines - 1, rows, width), BF16),
            vmem((rows, width), F32),
            dma((kinds, hops)), dma((kinds, hops)), dma((units, hops)), dma((units, hops)),
            dma((units,)), dma((units,)), dma((4,)), dma((4,)),
        ],
        compiler_params=pltpu.CompilerParams(
            collective_id=0, has_side_effects=True, vmem_limit_bytes=60 * 1024 * 1024
        ),
        cost_estimate=pl.CostEstimate(
            flops=12 * ticks * experts * tokens * width * ff, bytes_accessed=8 * width * ff, transcendentals=0
        ),
        name="window",
    )(
        acts.reshape(units, rows, width), carried.reshape(halves, rows, width),
        loss_grad.reshape(units, rows, width),
        jnp.swapaxes(expert_ids[0], 1, 2), jnp.swapaxes(probs[0], 1, 2), w_gate[0, 0], w_up[0, 0], w_down[0, 0],
    )
    down = down[:ff] + other_down.astype(F32)
    return out.reshape(1, ticks, tokens, width).astype(BF16), down.astype(BF16)[None, None]


def solution(mesh):
    return jax.shard_map(
        per_device,
        mesh=mesh,
        in_specs=(
            P("section", None, "expert", None),
            P("section", "expert", None),
            P(None, "expert", None),
            P("section", None, "expert", None),
            P("section", None, "expert", None),
            P("section", "expert", None, None),
            P("section", "expert", None, None),
            P("section", "expert", None, None),
        ),
        out_specs=(P("section", None, "expert", None), P("section", "expert", None, None)),
        check_vma=False,
    )
```

```python
import functools

import jax
import jax.numpy as jnp
from jax import lax
from jax.experimental import pallas as pl
from jax.experimental.pallas import tpu as pltpu
from jax.sharding import PartitionSpec as P

MESH = pl.DeviceIdType.MESH
BF16 = jnp.bfloat16
F32 = jnp.float32
HALVES = 2


def kernel(
    sections, lines,
    acts_ref, carried_ref, loss_ref, ids_ref, probs_ref, gate_ref, up_ref, down_ref,
    out_ref, down_out_ref,
    acts_all, inc_all, routed_all, gate_in, up_in, down_in, wide, wide_t, down_t, columns,
    steep, active_buf, hidden_buf, total, total_out, total_in,
    part, x_in, z_out, z_in, own_sum,
    ag_send, ag_recv, rs_send, rs_recv, relay_send, relay_recv, pair_send, pair_recv,
):
    units, tokens, width = acts_ref.shape
    halves = carried_ref.shape[0]
    blocks = 2 * lines
    count = blocks * tokens
    ff = gate_ref.shape[1]
    section = lax.axis_index("section")
    me = lax.axis_index("expert")
    a = me // 4
    b = lax.rem(me // 2, 2)
    c = lax.rem(me, 2)
    nb = 1 - b
    x_peer = a * 4 + nb * 2 + c
    core_peer = a * 4 + b * 2 + 1 - c
    is_last = section == sections - 1

    def line_at(j):
        return lax.rem(a + j, lines)

    def line_peer(j):
        return line_at(j) * 4 + b * 2 + c

    def line_back(j):
        return lax.rem(a + lines - j, lines)

    def gather_copy(buf, u, kind, index, where, target):
        ref = buf.at[b, where] if u is None else buf.at[u, b, where]
        return pltpu.make_async_remote_copy(
            src_ref=ref, dst_ref=ref,
            send_sem=ag_send.at[kind, index], recv_sem=ag_recv.at[kind, index],
            device_id={"expert": target}, device_id_type=MESH,
        )

    def z_copy(buf, u, kind, j):
        return gather_copy(buf, u, kind, j - 1, a, line_peer(j))

    def x_copy(buf, u, kind, j):
        return gather_copy(buf, u, kind, lines - 1 + j, line_back(j), x_peer)

    def gather_start(buf, u, kind):
        for j in range(1, lines):
            z_copy(buf, u, kind, j).start()
        x_copy(buf, u, kind, 0).start()

    def gather_lines(buf, u, kind):
        for j in range(1, lines):
            z_copy(buf, u, kind, j).wait_recv()
            x_copy(buf, u, kind, j).start()

    def gather_cross(buf, u, kind):
        for j in range(lines):
            x_copy(buf, u, kind, j).wait_recv()

    def gather_drain(buf, u, kind):
        for j in range(1, lines):
            z_copy(buf, u, kind, j).wait_send()
        for j in range(lines):
            x_copy(buf, u, kind, j).wait_send()

    def acts_kind(u):
        return 1 + u

    def inc_kind(u):
        return 1 + units + u

    def back_copy(u, index, src, dst, target):
        return pltpu.make_async_remote_copy(
            src_ref=src, dst_ref=dst,
            send_sem=rs_send.at[u, index], recv_sem=rs_recv.at[u, index],
            device_id={"expert": target}, device_id_type=MESH,
        )

    def back_x(u, j):
        return back_copy(u, j, part.at[u, nb, line_at(j)], x_in.at[u, line_at(j)], x_peer)

    def back_z(u, j):
        return back_copy(u, lines - 1 + j, z_out.at[u, j - 1], z_in.at[u, j - 1], line_peer(j))

    def relay(u):
        down_one = lax.rem(section + sections - 1, sections)
        return pltpu.make_async_remote_copy(
            src_ref=out_ref.at[u], dst_ref=inc_all.at[u + halves, b, a],
            send_sem=relay_send.at[u], recv_sem=relay_recv.at[u],
            device_id={"section": down_one}, device_id_type=MESH,
        )

    def pair_copy(index, src, dst):
        return pltpu.make_async_remote_copy(
            src_ref=src, dst_ref=dst, send_sem=pair_send.at[index], recv_sem=pair_recv.at[index],
            device_id={"expert": core_peer}, device_id_type=MESH,
        )

    swaps = [
        pair_copy(0, gate_ref, gate_in), pair_copy(1, up_ref, up_in),
        pair_copy(2, down_ref, down_in), pair_copy(3, total_out, total_in),
    ]

    barrier = pltpu.get_barrier_semaphore()
    for j in range(1, lines):
        pl.semaphore_signal(barrier, inc=1, device_id={"expert": line_peer(j)}, device_id_type=MESH)
    for peer in (x_peer, core_peer):
        pl.semaphore_signal(barrier, inc=1, device_id={"expert": peer}, device_id_type=MESH)
    for step in (1, sections - 1):
        other = lax.rem(section + step, sections)
        pl.semaphore_signal(barrier, inc=1, device_id={"section": other}, device_id_type=MESH)

    acts_all[:, b, a] = acts_ref[...]
    moments = range(ids_ref.shape[0])
    names = jnp.concatenate([ids_ref[t] for t in moments], axis=1)
    odds = jnp.concatenate([probs_ref[t] for t in moments], axis=1)
    expert_row = lax.broadcasted_iota(jnp.int32, (4 * lines, names.shape[1]), 0)
    routed = jnp.zeros(expert_row.shape, F32)
    for k in range(names.shape[0]):
        routed = routed + jnp.where(expert_row == names[k : k + 1, :], odds[k : k + 1, :], 0.0)
    routed_all[b, a] = routed

    @pl.when(is_last)
    def _():
        inc_all[:, b, a] = loss_ref[...]

    @pl.when(jnp.logical_not(is_last))
    def _():
        inc_all[:halves, b, a] = carried_ref[...]

    pl.semaphore_wait(barrier, lines + 3)

    def forward(u):
        start = pl.multiple_of(u * tokens, tokens)
        scales = []
        for i in range(2):
            table = columns[i, pl.ds(start, tokens), :]
            column = jnp.concatenate([table[:, p : p + 1] for p in range(blocks)], axis=0)
            scales.append(jnp.broadcast_to(column, (count, ff)))
        scale = jnp.concatenate(scales, axis=1)
        rows = acts_all[u].reshape(count, width)
        pre = jnp.dot(rows, wide[...], preferred_element_type=F32)
        gate_pre, up_pre = pre[:, : 2 * ff], pre[:, 2 * ff :]
        sigma = 1.0 / (1.0 + jnp.exp(-gate_pre))
        active = gate_pre * sigma
        hidden_buf[...] = (active * up_pre * scale).astype(BF16)
        steep[...] = up_pre * sigma * (1.0 + gate_pre * (1.0 - sigma)) * scale
        active_buf[...] = active * scale

    def backward(u):
        rows = inc_all[u].reshape(count, width)
        hidden_grad = jnp.dot(rows, down_t[...], preferred_element_type=F32)
        both = jnp.concatenate(
            [(hidden_grad * steep[...]).astype(BF16), (hidden_grad * active_buf[...]).astype(BF16)], axis=1
        )
        row_grad = jnp.dot(both, wide_t[...], preferred_element_type=F32)
        part[u] = row_grad.astype(BF16).reshape(2, lines, tokens, width)

    gather_start(routed_all, None, 0)
    gather_start(acts_all, 0, acts_kind(0))
    for swap in swaps[:3]:
        swap.start()
    gather_start(inc_all, 0, inc_kind(0))
    gather_start(acts_all, 1, acts_kind(1))
    wide[:, :ff] = gate_ref[...]
    wide[:, 2 * ff : 3 * ff] = up_ref[...]
    gather_lines(routed_all, None, 0)
    gather_lines(acts_all, 0, acts_kind(0))
    gather_lines(inc_all, 0, inc_kind(0))
    wide_t[:ff, :] = gate_ref[...].T
    wide_t[2 * ff : 3 * ff, :] = up_ref[...].T
    down_t[:, :ff] = down_ref[...].T
    gather_lines(acts_all, 1, acts_kind(1))
    total[...] = jnp.zeros_like(total)
    gather_cross(routed_all, None, 0)
    experts = 4 * lines
    table = routed_all[...].reshape(blocks, experts, units * tokens)
    names = lax.broadcasted_iota(jnp.int32, table.shape, 1)
    columns[0] = jnp.sum(jnp.where(names == me, table, 0.0), axis=1).T
    columns[1] = jnp.sum(jnp.where(names == core_peer, table, 0.0), axis=1).T
    swaps[0].wait_recv()
    wide[:, ff : 2 * ff] = gate_in[...]
    wide_t[ff : 2 * ff, :] = gate_in[...].T
    swaps[1].wait_recv()
    wide[:, 3 * ff :] = up_in[...]
    wide_t[3 * ff :, :] = up_in[...].T
    gather_cross(acts_all, 0, acts_kind(0))
    forward(0)
    swaps[2].wait_recv()
    down_t[:, ff:] = down_in[...].T
    gather_cross(inc_all, 0, inc_kind(0))

    def step(u, carry):
        more = u + 1 < units
        more_two = u + 2 < units
        backward(u)
        for j in range(lines):
            back_x(u, j).start()

        @pl.when(more)
        def _():
            @pl.when(jnp.logical_and(u + 1 >= halves, jnp.logical_not(is_last)))
            def _():
                relay(u + 1 - halves).wait_recv()

            gather_start(inc_all, u + 1, inc_kind(u + 1))

        @pl.when(more_two)
        def _():
            gather_start(acts_all, u + 2, acts_kind(u + 2))

        total[...] += lax.dot_general(
            hidden_buf[...], inc_all[u].reshape(count, width), (((0,), (0,)), ((), ())),
            preferred_element_type=F32,
        )

        @pl.when(more)
        def _():
            gather_cross(acts_all, u + 1, acts_kind(u + 1))
            forward(u + 1)
            gather_lines(inc_all, u + 1, inc_kind(u + 1))

        for j in list(range(1, lines)) + [0]:
            back_x(u, j).wait_recv()
            where = line_at(j)
            quad = part[u, b, where].astype(F32) + x_in[u, where].astype(F32)
            if j:
                z_out[u, j - 1] = quad.astype(BF16)
                back_z(u, j).start()
            else:
                own_sum[...] = quad + inc_all[u, b, a].astype(F32)

        @pl.when(more_two)
        def _():
            gather_lines(acts_all, u + 2, acts_kind(u + 2))

        @pl.when(jnp.logical_not(more))
        def _():
            total_out[...] = total[ff:, :].astype(BF16)
            swaps[3].start()

        result = own_sum[...]
        for j in range(1, lines):
            back_z(u, j).wait_recv()
            result = result + z_in[u, j - 1].astype(F32)
        out_ref[u] = result.astype(BF16)

        @pl.when(jnp.logical_and(u + halves < units, section > 0))
        def _():
            relay(u).start()

        @pl.when(more)
        def _():
            gather_cross(inc_all, u + 1, inc_kind(u + 1))

        return carry

    lax.fori_loop(0, units, step, 0)
    swaps[3].wait_recv()
    down_out_ref[...] = (total[:ff, :] + total_in[...].astype(F32)).astype(BF16)
    gather_drain(routed_all, None, 0)
    for swap in swaps:
        swap.wait_send()

    def drain(u, carry):
        gather_drain(acts_all, u, acts_kind(u))
        gather_drain(inc_all, u, inc_kind(u))
        for j in range(lines):
            back_x(u, j).wait_send()
        for j in range(1, lines):
            back_z(u, j).wait_send()

        @pl.when(jnp.logical_and(u + halves < units, section > 0))
        def _():
            relay(u).wait_send()

        return carry

    lax.fori_loop(0, units, drain, 0)


def per_device(acts, carried, loss_grad, expert_ids, probs, w_gate, w_up, w_down):
    sections = lax.axis_size("section")
    experts = lax.axis_size("expert")
    lines = experts // 4
    ticks, tokens, width = acts.shape[1:]
    ff = w_gate.shape[3]
    halves = HALVES
    units, rows = ticks * halves, tokens // halves
    kinds, hops = 1 + 2 * units, 2 * lines - 1
    count = 2 * lines * rows
    dma = pltpu.SemaphoreType.DMA
    vmem = pltpu.VMEM
    gathered = (units, 2, lines, rows, width)
    out, down = pl.pallas_call(
        functools.partial(kernel, sections, lines),
        out_shape=(
            jax.ShapeDtypeStruct((units, rows, width), BF16),
            jax.ShapeDtypeStruct((ff, width), BF16),
        ),
        in_specs=[pl.BlockSpec(memory_space=vmem)] * 8,
        out_specs=(pl.BlockSpec(memory_space=vmem),) * 2,
        scratch_shapes=[
            vmem(gathered, BF16), vmem(gathered, BF16), vmem((2, lines, experts, ticks * tokens), F32),
            vmem((width, ff), BF16), vmem((width, ff), BF16), vmem((ff, width), BF16),
            vmem((width, 4 * ff), BF16), vmem((4 * ff, width), BF16), vmem((width, 2 * ff), BF16),
            vmem((2, ticks * tokens, 2 * lines), F32),
            vmem((count, 2 * ff), F32), vmem((count, 2 * ff), F32), vmem((count, 2 * ff), BF16),
            vmem((2 * ff, width), F32), vmem((ff, width), BF16), vmem((ff, width), BF16),
            vmem(gathered, BF16), vmem((units, lines, rows, width), BF16),
            vmem((units, lines - 1, rows, width), BF16), vmem((units, lines - 1, rows, width), BF16),
            vmem((rows, width), F32),
            dma((kinds, hops)), dma((kinds, hops)), dma((units, hops)), dma((units, hops)),
            dma((units,)), dma((units,)), dma((4,)), dma((4,)),
        ],
        compiler_params=pltpu.CompilerParams(
            collective_id=0, has_side_effects=True, vmem_limit_bytes=60 * 1024 * 1024
        ),
        cost_estimate=pl.CostEstimate(
            flops=12 * ticks * experts * tokens * width * ff, bytes_accessed=8 * width * ff, transcendentals=0
        ),
        name="window",
    )(
        acts.reshape(units, rows, width), carried.reshape(halves, rows, width),
        loss_grad.reshape(units, rows, width),
        jnp.swapaxes(expert_ids[0], 1, 2), jnp.swapaxes(probs[0], 1, 2), w_gate[0, 0], w_up[0, 0], w_down[0, 0],
    )
    return out.reshape(1, ticks, tokens, width), down[None, None]


def solution(mesh):
    return jax.shard_map(
        per_device,
        mesh=mesh,
        in_specs=(
            P("section", None, "expert", None),
            P("section", "expert", None),
            P(None, "expert", None),
            P("section", None, "expert", None),
            P("section", None, "expert", None),
            P("section", "expert", None, None),
            P("section", "expert", None, None),
            P("section", "expert", None, None),
        ),
        out_specs=(P("section", None, "expert", None), P("section", "expert", None, None)),
        check_vma=False,
    )
```
